32 devices in a mesh: shard: 8 (over z, y), rep: 4 (over x, core).
Axes of the slice: x: 2, y: 2, z: 4, core: 2. Of those that a mesh axis runs over, the one named last changes fastest.
Arguments:
- tokens: bfloat16 [32768, 768], P(('shard', 'rep')), may hold values from -6 to 6
- lengths: int32 [32], P(('shard', 'rep')), may hold values from 1 to 1024, 24576 in all
- expert_choice: int32 [32768, 1], P(('shard', 'rep')), may hold values from 0 to 7
- query_weight: bfloat16 [768, 768], P('shard'), may hold values from -0.21875 to 0.21875
- key_weight: bfloat16 [768, 768], P('shard'), may hold values from -0.21875 to 0.21875
- value_weight: bfloat16 [768, 768], P('shard'), may hold values from -0.21875 to 0.21875
- output_weight: bfloat16 [768, 768], P('shard'), may hold values from -3.5 to 3.5
- first_gain: bfloat16 [768], P('shard'), may hold values from 0.5 to 1.5
- second_gain: bfloat16 [768], P('shard'), may hold values from 0.5 to 1.5
- router_weight: bfloat16 [768, 8], P('shard'), may hold values from -0.15625 to 0.15625
- bias_table: bfloat16 [32, 12], P('shard'), may hold values from -4 to 4
- expert_in: bfloat16 [8, 768, 3072], P('shard'), may hold values from -0.21875 to 0.21875
- expert_out: bfloat16 [8, 3072, 768], P('shard'), may hold values from -0.875 to 0.875
- cotangent: bfloat16 [32768, 768], P(('shard', 'rep')), may hold values from -6 to 6
Outputs:
- layer_out: bfloat16 [32768, 768], P(('shard', 'rep'))
- token_grad: bfloat16 [32768, 768], P(('shard', 'rep'))
- query_weight_grad: float32 [768, 768], P('shard')
- key_weight_grad: float32 [768, 768], P('shard')
- value_weight_grad: float32 [768, 768], P('shard')
- output_weight_grad: float32 [768, 768], P('shard')
- first_gain_grad: float32 [768], P('shard')
- second_gain_grad: float32 [768], P('shard')
- router_weight_grad: float32 [768, 8], P('shard')
- bias_table_grad: float32 [32, 12], P('shard')
- expert_in_grad: float32 [8, 768, 3072], P('shard')
- expert_out_grad: float32 [8, 3072, 768], P('shard')
The draws below stay inside these ranges and needn't reach their ends.
Inputs may be any that keep to these rules, and one draw needn't show every extreme that they name: `lengths`: some sequence is 1024 tokens long. `expert_choice`: every expert is chosen by some token.
All inputs are finite; a program needn't handle non-finite values. No bound on the sum of `lengths` on one device may be relied on, other than what follows from the above.
Results may differ from the reference program's by a relative error of at most 0.02.
Values may be sent and summed in bfloat16 or wider, within the bound.
A program may use at most 320 MiB of HBM per device.

```python
import math
from functools import partial
import jax
import jax.numpy as jnp
import numpy as np
from jax import lax

D = 768
HEADS = 12
HEAD_DIM = 64
FF = 3072
BUCKETS = 32
MAX_DISTANCE = 128
TOK_DEV = 1024
SEQS = 32
TOKENS = 32768
EXPERTS = 8
CAPACITY = 128


def level_of(rng, extent, split, least, top_value):
    factor_of, own = 1.0, jax.random.fold_in(rng, 6)
    for position, parts in split:
        draws = jnp.exp(jax.random.uniform(jax.random.fold_in(own, position), (parts,), jnp.float32, least / len(split), top_value / len(split)))
        factor_of = factor_of * jnp.repeat(draws, extent[position] // parts).reshape([-1 if axis == position else 1 for axis in range(len(extent))])
    return factor_of


def distinct(rng, rows, amount, top, lift):
    ranking = jax.random.permutation(jax.random.fold_in(rng, 1), amount)
    boost = ranking
    for power in range(3):
        boost = boost * boost // amount
    boost = boost * lift // amount
    chance = jax.random.randint(jax.random.fold_in(rng, 2), (rows, amount), 0, 4096) + boost
    fixed_rows = jax.random.permutation(jax.random.fold_in(rng, 3), rows)[jnp.arange(amount) % rows]
    chance = jnp.where(jnp.arange(rows)[:, None] == fixed_rows[None, :], 1 << 14, chance)
    priority = chance * amount + jnp.arange(amount)
    return lax.top_k(priority.astype(jnp.int32), top)[1].astype(jnp.int32)


def length_profile(number_of, total, most, skew):
    portions = [(1 << 20) // math.isqrt(rank ** skew) + 1 for rank in range(2, number_of + 1)]
    surplus, given = total - most - (number_of - 1), [1] * (number_of - 1)
    while surplus > 0:
        free = [i for i in range(number_of - 1) if given[i] < most]
        pool, left = sum([portions[i] for i in free]), surplus
        for i in free:
            extra = min(most - given[i], max(1, left * portions[i] // pool), surplus)
            given[i] = given[i] + extra
            surplus = surplus - extra
    return np.array([most] + given)


def ragged(stream_key, number_of, total, limit, slope):
    if number_of == 2:
        one = jax.random.randint(stream_key, (), max(1, total - limit), min(limit, total - 1) + 1)
        return jnp.stack([one, total - one])
    tallies = jnp.asarray(length_profile(number_of, total, limit, slope), jnp.int32)
    twos = (number_of - 1) // 2
    donor, receiver = tallies[1:1 + 2 * twos:2], tallies[2:2 + 2 * twos:2]
    margin = jnp.minimum(donor - 1, limit - receiver)
    passed = jax.random.randint(jax.random.fold_in(stream_key, 1), (twos,), 0, 1 << 20) % (margin + 1)
    tallies = tallies.at[1:1 + 2 * twos:2].set(donor - passed).at[2:2 + 2 * twos:2].set(receiver + passed)
    return tallies[jax.random.permutation(jax.random.fold_in(stream_key, 2), number_of)]


def noise(stream_key, shape, width, limit, cuts=(), kind=jnp.bfloat16):
    drawn = jax.random.normal(stream_key, shape, jnp.float32) * width
    if len(cuts) > 0:
        drawn = level_of(stream_key, shape, cuts, -0.22, 0.18) * drawn
    return jnp.clip(drawn, min=-limit, max=limit).astype(kind)


def setup_inputs(seed: int = 0) -> dict:
    key_of = jax.random.split(jax.random.key(seed), 15)
    return {
        "tokens": noise(key_of[0], (TOKENS, D), 1.0, 6.0, ((0, 32),)),
        "lengths": ragged(key_of[1], SEQS, SEQS * TOK_DEV * 3 // 4, TOK_DEV, 1).astype(jnp.int32),
        "expert_choice": distinct(key_of[2], TOKENS, EXPERTS, 1, 1024),
        "query_weight": noise(key_of[3], (D, D), D ** -0.5, 0.21875, ((0, 8),)),
        "key_weight": noise(key_of[4], (D, D), D ** -0.5, 0.21875, ((0, 8),)),
        "value_weight": noise(key_of[5], (D, D), D ** -0.5, 0.21875, ((0, 8),)),
        "output_weight": noise(key_of[6], (D, D), (max(D // 256, 1)) ** -0.5, 3.5, ((0, 8),)),
        "first_gain": jnp.clip(1.0 + 0.1 * jax.random.normal(key_of[7], (D,), jnp.float32), 0.5, 1.5).astype(jnp.bfloat16),
        "second_gain": jnp.clip(1.0 + 0.1 * jax.random.normal(key_of[8], (D,), jnp.float32), 0.5, 1.5).astype(jnp.bfloat16),
        "router_weight": noise(key_of[9], (D, EXPERTS), (2 * D) ** -0.5, 0.15625, ((0, 8),)),
        "bias_table": noise(key_of[10], (BUCKETS, HEADS), 1.0, 4.0, ((0, 8),)),
        "expert_in": noise(key_of[11], (EXPERTS, D, FF), D ** -0.5, 0.21875, ((0, 8),)),
        "expert_out": noise(key_of[12], (EXPERTS, FF, D), (max(FF // (EXPERTS * EXPERTS), 1)) ** -0.5, 0.875, ((0, 8),)),
        "cotangent": noise(key_of[13], (TOKENS, D), 1.0, 6.0, ((0, 32),)),
    }


EPSILON = 1e-06
PRECISE = lax.Precision.HIGHEST
MASKED = -1000000000.0

@jax.custom_vjp
def low(v):
    return lax.optimization_barrier(v.astype(jnp.bfloat16)).astype(jnp.float32)

@jax.custom_vjp
def low_back(v):
    return v

def low_keep(v):
    return (low(v), None)

def low_pass(kept, grad):
    return (grad,)

def back_keep(v):
    return (v, None)

def back_low(kept, grad):
    return (low(grad),)
low.defvjp(low_keep, low_pass)
low_back.defvjp(back_keep, back_low)

def bucket_rows(slot_count, bucket_count, reach):
    offset_list = np.arange(-(slot_count - 1), slot_count)
    half_count = bucket_count // 2
    exact_count = half_count // 2
    upper_part = (offset_list > 0).astype(np.int64) * half_count
    distance = np.abs(offset_list)
    spread_log = np.log(np.maximum(distance, 1) / exact_count) / np.log(reach / exact_count) * (half_count - exact_count)
    far_bucket = np.minimum(exact_count + np.maximum(spread_log, 0.0).astype(np.int64), half_count - 1)
    bucket_ids = upper_part + np.where(distance < exact_count, distance, far_bucket)
    return (bucket_ids[:, None] == np.arange(bucket_count)[None, :]).astype(np.float32)

def spread_index(first_row, block_rows, slot_count):
    return np.arange(slot_count)[None, :] - np.arange(first_row, first_row + block_rows)[:, None] + slot_count - 1

def rms(values, gain):
    inverse = lax.rsqrt(lax.optimization_barrier(jnp.mean(values * values, axis=-1, keepdims=True)) + EPSILON)
    return values * inverse * gain

def attend_sequence(member, bias):
    query_part, key_part, value_part, length = member
    scores = jnp.einsum('qhd,khd->hqk', query_part, key_part, precision=PRECISE) * 0.125 + bias
    valid = jnp.arange(TOK_DEV, dtype=jnp.int32) < length
    scores = low_back(jnp.where(valid[None, None, :], scores, MASKED))
    probs = low(jax.nn.softmax(scores, axis=-1))
    return jnp.einsum('hqk,khd->qhd', probs, value_part, precision=PRECISE)

def expert_rows(member):
    rows_here, weight_in, weight_out = member
    inner = low_back(jnp.dot(rows_here, weight_in, precision=PRECISE))
    active = low(jax.nn.gelu(inner))
    return low(low_back(jnp.dot(active, weight_out, precision=PRECISE)))

def forward(inputs, query_weight, key_weight, value_weight, output_weight, first_gain, second_gain, router_weight, bias_table, expert_in, expert_out, lengths, rows_index, rows_valid, choice_hot):
    normed = low(rms(inputs, first_gain))
    queries = low(low_back(jnp.dot(normed, query_weight, precision=PRECISE)))
    keys_all = low(low_back(jnp.dot(normed, key_weight, precision=PRECISE)))
    values_all = low(low_back(jnp.dot(normed, value_weight, precision=PRECISE)))
    offsets = jnp.dot(jnp.asarray(bucket_rows(TOK_DEV, BUCKETS, MAX_DISTANCE)), bias_table, precision=PRECISE).T
    bias = jnp.take(offsets, jnp.asarray(spread_index(0, TOK_DEV, TOK_DEV)), axis=1)
    seq_shape = (SEQS, TOK_DEV, HEADS, HEAD_DIM)
    mixed = lax.map(jax.checkpoint(partial(attend_sequence, bias=bias)), (queries.reshape(seq_shape), keys_all.reshape(seq_shape), values_all.reshape(seq_shape), lengths))
    attended = low(low_back(mixed.reshape(TOKENS, D)))
    middle = inputs + low_back(jnp.dot(attended, output_weight, precision=PRECISE))
    second = low(rms(middle, second_gain))
    logits = low_back(jnp.dot(second, router_weight, precision=PRECISE))
    router_probs = jax.nn.softmax(logits, axis=-1)
    gates = lax.optimization_barrier(jnp.sum(jnp.where(choice_hot, router_probs, 0.0), axis=-1))
    picked_rows = jnp.take(second, jnp.minimum(rows_index, TOKENS - 1), axis=0) * rows_valid[:, None]
    slot_rows = low_back(picked_rows).reshape(EXPERTS, SEQS * CAPACITY, D)
    results = lax.map(jax.checkpoint(expert_rows), (slot_rows, expert_in, expert_out))
    flat_results = results.reshape(EXPERTS * SEQS * CAPACITY, D) * rows_valid[:, None]
    combined = jnp.zeros((TOKENS, D), jnp.float32).at[rows_index].add(flat_results, mode='drop')
    return middle + gates[:, None] * combined

def reference(tokens, lengths, expert_choice, query_weight, key_weight, value_weight, output_weight, first_gain, second_gain, router_weight, bias_table, expert_in, expert_out, cotangent):
    live = jnp.arange(TOK_DEV, dtype=jnp.int32)[None, :] < lengths[:, None]
    chosen = expert_choice.reshape(SEQS, TOK_DEV)
    expert_ids = jnp.arange(EXPERTS, dtype=jnp.int32)
    hot_live = ((chosen[:, :, None] == expert_ids[None, None, :]) & live[:, :, None]).astype(jnp.int32)
    before = (jnp.cumsum(hot_live, axis=1) - hot_live).astype(jnp.int32)
    slot = lax.optimization_barrier(jnp.sum(before * hot_live, axis=2)).astype(jnp.int32)
    kept = live & (slot < CAPACITY)
    block_ids = jnp.arange(SEQS, dtype=jnp.int32)[:, None]
    linear = ((chosen * SEQS + block_ids) * CAPACITY + slot).astype(jnp.int32)
    linear = jnp.where(kept, linear, EXPERTS * SEQS * CAPACITY).astype(jnp.int32).reshape(TOKENS)
    rows_index = jnp.full((EXPERTS * SEQS * CAPACITY,), TOKENS, jnp.int32).at[linear].set(jnp.arange(TOKENS, dtype=jnp.int32), mode='drop')
    rows_valid = (rows_index < TOKENS).astype(jnp.float32)
    choice_hot = expert_choice == expert_ids[None, :]
    bound = partial(forward, lengths=lengths, rows_index=rows_index, rows_valid=rows_valid, choice_hot=choice_hot)
    layer, pull = jax.vjp(bound, tokens.astype(jnp.float32), query_weight.astype(jnp.float32), key_weight.astype(jnp.float32), value_weight.astype(jnp.float32), output_weight.astype(jnp.float32), first_gain.astype(jnp.float32), second_gain.astype(jnp.float32), router_weight.astype(jnp.float32), bias_table.astype(jnp.float32), expert_in.astype(jnp.float32), expert_out.astype(jnp.float32))
    upstream = cotangent.astype(jnp.float32) * live.reshape(TOKENS)[:, None].astype(jnp.float32)
    grads = pull(upstream)
    return (layer.astype(jnp.bfloat16), grads[0].astype(jnp.bfloat16), grads[1], grads[2], grads[3], grads[4], grads[5], grads[6], grads[7], grads[8], grads[9], grads[10])
```

```python
import jax
import jax.numpy as jnp
import numpy as np
from jax import lax
from jax.experimental import pallas as pl
from jax.experimental.pallas import tpu as pltpu
from jax.sharding import PartitionSpec as P

MAX_DISTANCE = 128
EPSILON = 1e-06
MASKED = -1000000000.0
TILE = 128
QUERY_BLOCK = 256


def contract(left_side, right_side, left_axis, right_axis):
    return lax.dot_general(
        left_side,
        right_side,
        (((left_axis,), (right_axis,)), ((), ())),
        preferred_element_type=jnp.float32,
    )


def offset_buckets(bucket_count, reach):
    half_count = bucket_count // 2
    exact_count = half_count // 2
    offset_list = -(np.arange(4 * TILE) - 2 * TILE)
    distance = np.abs(offset_list)
    spread_log = (
        np.log(np.maximum(distance, 1) / exact_count)
        / np.log(reach / exact_count)
        * (half_count - exact_count)
    )
    far_bucket = np.minimum(
        exact_count + np.maximum(spread_log, 0.0).astype(np.int64), half_count - 1
    )
    return (offset_list > 0) * half_count + np.where(
        distance < exact_count, distance, far_bucket
    )


def fill_strip(strip_ref, offsets, slot_count):
    base = slot_count - TILE
    wide = pltpu.roll(
        jnp.broadcast_to(offsets, (TILE, 4 * TILE)), 0, 1, stride=1, stride_axis=0
    )
    strip_ref[: base - TILE, :] = jnp.broadcast_to(
        offsets[:, 4 * TILE - 1 : 4 * TILE], (base - TILE, TILE)
    )
    for shift in (-1, 0, 1):
        first = (2 - shift) * TILE
        row = base + shift * TILE
        strip_ref[row : row + TILE, :] = wide[:, first : first + TILE]
    strip_ref[base + 2 * TILE :, :] = jnp.broadcast_to(
        offsets[:, 0:1], (slot_count - 2 * TILE, TILE)
    )


def biased(strip_ref, scores, first_row, slot_count):
    parts = []
    for part in range(QUERY_BLOCK // TILE):
        start = slot_count - TILE - first_row - part * TILE
        parts.append(
            scores[:, part * TILE : (part + 1) * TILE]
            + strip_ref[start : start + slot_count, :]
        )
    return jnp.concatenate(parts, axis=1)


def attend_kernel(q_ref, k_ref, v_ref, mask_ref, offset_ref, out_ref, log_ref, strip_ref):
    slot_count, width = q_ref.shape
    head_size = width // 2
    lane = lax.broadcasted_iota(jnp.int32, (QUERY_BLOCK, width), 1)
    one_lane = (lane == 0).astype(jnp.bfloat16)
    keys = jnp.concatenate([k_ref[...], mask_ref[...]], axis=1)
    values_turned = jnp.concatenate(
        [v_ref[...].T, jnp.ones((16, slot_count), jnp.bfloat16)], axis=0
    )
    for half in range(2):
        fill_strip(strip_ref.at[half], offset_ref[0, half : half + 1, :], slot_count)
    for first_row in range(0, slot_count, QUERY_BLOCK):
        rows = slice(first_row, first_row + QUERY_BLOCK)
        q_block = q_ref[rows, :] * jnp.bfloat16(0.125)
        pieces = []
        for half in range(2):
            mine = (lane // head_size) == half
            q_half = jnp.concatenate(
                [jnp.where(mine, q_block, jnp.bfloat16(0)), one_lane], axis=1
            )
            scores = biased(strip_ref.at[half], contract(keys, q_half, 1, 1), first_row, slot_count)
            peak = jnp.max(scores, axis=0, keepdims=True)
            weights = jnp.exp(scores - peak).astype(jnp.bfloat16)
            mixed = jnp.dot(values_turned, weights, preferred_element_type=jnp.float32)
            total = mixed[width : width + 1, :]
            pieces.append(mixed[half * head_size : (half + 1) * head_size, :] / total)
            log_ref[0, half : half + 1, rows] = peak + jnp.log(total)
        out_ref[rows, :] = jnp.concatenate(pieces, axis=0).T.astype(jnp.bfloat16)


def attend_back_kernel(
    q_ref, k_ref, v_ref, mask_ref, offset_ref, log_ref, out_ref, grad_ref,
    dq_ref, dk_ref, dv_ref, table_ref, strip_ref, sum_ref,
):
    slot_count, width = q_ref.shape
    head_size = width // 2
    lane = lax.broadcasted_iota(jnp.int32, (QUERY_BLOCK, width), 1)
    one_lane = (lane == 0).astype(jnp.bfloat16)
    keys = jnp.concatenate([k_ref[...], mask_ref[...]], axis=1)
    keys_turned = k_ref[...].T
    values = v_ref[...]
    for half in range(2):
        fill_strip(strip_ref.at[half], offset_ref[0, half : half + 1, :], slot_count)
    sum_ref[...] = jnp.zeros(sum_ref.shape, jnp.float32)
    key_total = jnp.zeros((slot_count, width), jnp.float32)
    value_total = jnp.zeros((slot_count, width), jnp.float32)
    for first_row in range(0, slot_count, QUERY_BLOCK):
        rows = slice(first_row, first_row + QUERY_BLOCK)
        q_block = q_ref[rows, :] * jnp.bfloat16(0.125)
        grad_block = grad_ref[rows, :]
        product = (
            grad_block.astype(jnp.float32) * out_ref[rows, :].astype(jnp.float32)
        ).T
        pieces = []
        weights_parts, score_parts, q_parts, grad_parts = [], [], [], []
        for half in range(2):
            mine = (lane // head_size) == half
            q_own = jnp.where(mine, q_block, jnp.bfloat16(0))
            grad_own = jnp.where(mine, grad_block, jnp.bfloat16(0))
            delta = jnp.sum(
                product[half * head_size : (half + 1) * head_size, :], axis=0, keepdims=True
            )
            q_half = jnp.concatenate([q_own, one_lane], axis=1)
            scores = biased(strip_ref.at[half], contract(keys, q_half, 1, 1), first_row, slot_count)
            weights = jnp.exp(scores - log_ref[0, half : half + 1, rows])
            prob_grad = contract(values, grad_own, 1, 1)
            score_grad = weights * (prob_grad - delta)
            for part in range(QUERY_BLOCK // TILE):
                start = slot_count - TILE - first_row - part * TILE
                sum_ref[half, start : start + slot_count, :] += score_grad[
                    :, part * TILE : (part + 1) * TILE
                ]
            score_low = score_grad.astype(jnp.bfloat16)
            turned = jnp.dot(keys_turned, score_low, preferred_element_type=jnp.float32)
            pieces.append(turned[half * head_size : (half + 1) * head_size, :] * 0.125)
            weights_parts.append(weights.astype(jnp.bfloat16))
            score_parts.append(score_low)
            q_parts.append(q_own)
            grad_parts.append(grad_own)
        dq_ref[rows, :] = jnp.concatenate(pieces, axis=0).T.astype(jnp.bfloat16)
        key_total = key_total + jnp.dot(
            jnp.concatenate(score_parts, axis=1),
            jnp.concatenate(q_parts, axis=0),
            preferred_element_type=jnp.float32,
        )
        value_total = value_total + jnp.dot(
            jnp.concatenate(weights_parts, axis=1),
            jnp.concatenate(grad_parts, axis=0),
            preferred_element_type=jnp.float32,
        )
    dk_ref[...] = key_total.astype(jnp.bfloat16)
    dv_ref[...] = value_total.astype(jnp.bfloat16)
    base = slot_count - TILE
    table_ref[...] = jnp.zeros(table_ref.shape, jnp.float32)
    for half in range(2):
        sums = sum_ref.at[half]
        wide = jnp.concatenate(
            [jnp.zeros((TILE, TILE), jnp.float32)]
            + [sums[base + shift * TILE : base + (shift + 1) * TILE, :] for shift in (1, 0, -1)],
            axis=1,
        )
        level = wide
        row = lax.broadcasted_iota(jnp.int32, wide.shape, 0)
        amount = 1
        while amount < TILE:
            level = jnp.where(
                (row // amount) % 2 == 1, pltpu.roll(level, 4 * TILE - amount, 1), level
            )
            amount *= 2
        table_ref[0, half : half + 1, :] = jnp.sum(level, axis=0, keepdims=True)
        far_left = jnp.sum(sums[: base - TILE, :], axis=0, keepdims=True)
        far_right = jnp.sum(sums[base + 2 * TILE :, :], axis=0, keepdims=True)
        table_ref[0, 2 + half : 3 + half, :] = jnp.concatenate(
            [far_left, far_right, jnp.zeros((1, 2 * TILE), jnp.float32)], axis=1
        )


def pair_specs(slot_count):
    column = pl.BlockSpec((slot_count, 2 * 64), lambda p: (0, p))
    mask = pl.BlockSpec((slot_count, TILE), lambda p: (0, 0))
    small = lambda rows, lanes: pl.BlockSpec((1, rows, lanes), lambda p: (p, 0, 0))
    return column, mask, small


def attend(queries, keys, values, mask, offsets):
    slot_count, model_width = queries.shape
    pairs = offsets.shape[0]
    column, mask_spec, small = pair_specs(slot_count)
    strip = pltpu.VMEM((2, 2 * slot_count - TILE, TILE), jnp.float32)
    return pl.pallas_call(
        attend_kernel,
        grid=(pairs,),
        in_specs=[column, column, column, mask_spec, small(2, 4 * TILE)],
        out_specs=[column, small(2, slot_count)],
        out_shape=[
            jax.ShapeDtypeStruct((slot_count, model_width), jnp.bfloat16),
            jax.ShapeDtypeStruct((pairs, 2, slot_count), jnp.float32),
        ],
        scratch_shapes=[strip],
        compiler_params=pltpu.CompilerParams(vmem_limit_bytes=50 * 2**20),
        cost_estimate=pl.CostEstimate(
            flops=2 * pairs * slot_count * slot_count * 800,
            bytes_accessed=8 * slot_count * model_width,
            transcendentals=2 * pairs * slot_count * slot_count,
        ),
        name="attend",
    )(queries, keys, values, mask, offsets)


def attend_back(queries, keys, values, mask, offsets, logs, attended, grad):
    slot_count, model_width = queries.shape
    pairs = offsets.shape[0]
    column, mask_spec, small = pair_specs(slot_count)
    strip = pltpu.VMEM((2, 2 * slot_count - TILE, TILE), jnp.float32)
    wide = jax.ShapeDtypeStruct((slot_count, model_width), jnp.bfloat16)
    return pl.pallas_call(
        attend_back_kernel,
        grid=(pairs,),
        in_specs=[
            column, column, column, mask_spec, small(2, 4 * TILE), small(2, slot_count),
            column, column,
        ],
        out_specs=[column, column, column, small(4, 4 * TILE)],
        out_shape=[
            wide, wide, wide, jax.ShapeDtypeStruct((pairs, 4, 4 * TILE), jnp.float32)
        ],
        scratch_shapes=[strip, strip],
        compiler_params=pltpu.CompilerParams(vmem_limit_bytes=56 * 2**20),
        cost_estimate=pl.CostEstimate(
            flops=2 * pairs * slot_count * slot_count * 1600,
            bytes_accessed=16 * slot_count * model_width,
            transcendentals=2 * pairs * slot_count * slot_count,
        ),
        name="attend_back",
    )(queries, keys, values, mask, offsets, logs, attended, grad)


def spread_table(table):
    bucket_count, head_count = table.shape
    hot = (
        offset_buckets(bucket_count, MAX_DISTANCE)[None, :] == np.arange(bucket_count)[:, None]
    )
    spread = contract(table, jnp.asarray(hot, jnp.bfloat16), 0, 0)
    return spread.reshape(head_count // 2, 2, 4 * TILE)


def collect_table(sums, bucket_count):
    pairs = sums.shape[0]
    buckets = offset_buckets(bucket_count, MAX_DISTANCE)
    near = sums[:, :2, :].reshape(2 * pairs, 4 * TILE)
    far = sums[:, 2:, : 2 * TILE].reshape(2 * pairs, 2 * TILE)
    hot = buckets[:, None] == np.arange(bucket_count)[None, :]
    far_buckets = np.where(np.arange(2 * TILE) < TILE, buckets[-1], buckets[0])
    far_hot = far_buckets[:, None] == np.arange(bucket_count)[None, :]
    both = jnp.concatenate([near, far], axis=1)
    both_hot = jnp.asarray(np.concatenate([hot, far_hot], axis=0), jnp.float32)
    return lax.dot_general(
        both_hot, both, (((0,), (1,)), ((), ())), precision=lax.Precision.HIGHEST,
        preferred_element_type=jnp.float32,
    )


def rms_forward(values, gain):
    inverse = lax.rsqrt(jnp.mean(values * values, axis=-1, keepdims=True) + EPSILON)
    return (values * inverse * gain, inverse)


def rms_backward(values, inverse, gain, upstream):
    scaled = upstream * gain
    gain_grad = jnp.sum(upstream * values * inverse, axis=0)
    inner_mean = jnp.mean(scaled * values, axis=-1, keepdims=True)
    return (inverse * scaled - values * inverse * inverse * inverse * inner_mean, gain_grad)


def pack_small(parts, width):
    flat = jnp.concatenate([part.reshape(-1) for part in parts])
    rows = -(-flat.shape[0] // width)
    return jnp.pad(flat, (0, rows * width - flat.shape[0])).reshape(rows, width)


def gather_packed(packed, group_size):
    replicas = lax.axis_size("rep")
    rows, width = packed.shape
    part = -(-rows // replicas)
    packed = jnp.pad(packed, ((0, part * replicas - rows), (0, 0)))
    own = lax.dynamic_slice_in_dim(packed, lax.axis_index("rep") * part, part, 0)
    whole = lax.all_gather(own, ("shard", "rep"), axis=0)
    return whole.reshape(group_size, part * replicas, width)[:, :rows]


def replica_sum(value):
    return lax.psum(value, "rep")


def on_device(
    tokens,
    lengths,
    expert_choice,
    query_weight,
    key_weight,
    value_weight,
    output_weight,
    first_gain,
    second_gain,
    router_weight,
    bias_table,
    expert_in,
    expert_out,
    cotangent,
):
    token_count, model_width = tokens.shape
    group_size = lax.axis_size("shard")
    expert_count = router_weight.shape[1]
    capacity = token_count // group_size
    bucket_count = bias_table.shape[0] * group_size
    shard_rows = query_weight.shape[0]
    live_mask = jnp.arange(token_count, dtype=jnp.int32) < lengths[0]
    small_parts = (router_weight, first_gain, second_gain, bias_table)
    packed = jnp.concatenate(
        [
            query_weight,
            key_weight,
            value_weight,
            output_weight,
            pack_small(small_parts, model_width),
        ],
        axis=0,
    )
    whole = gather_packed(packed, group_size)
    full_query, full_key, full_value, full_output = (
        whole[:, index * shard_rows : (index + 1) * shard_rows].reshape(-1, model_width)
        for index in range(4)
    )
    small = whole[:, 4 * shard_rows :].reshape(group_size, -1)
    unpacked = []
    position = 0
    for part in small_parts:
        unpacked.append(
            small[:, position : position + part.size].reshape((-1,) + part.shape[1:])
        )
        position += part.size
    full_router, first_low, second_low_gain, table_low = unpacked
    first_scale = first_low.astype(jnp.float32)
    second_scale = second_low_gain.astype(jnp.float32)
    inputs = tokens.astype(jnp.float32)
    normed, first_inverse = rms_forward(inputs, first_scale)
    normed_low = normed.astype(jnp.bfloat16)
    queries = jnp.dot(normed_low, full_query, preferred_element_type=jnp.float32).astype(
        jnp.bfloat16
    )
    keys_low = jnp.dot(normed_low, full_key, preferred_element_type=jnp.float32).astype(
        jnp.bfloat16
    )
    values_low = jnp.dot(normed_low, full_value, preferred_element_type=jnp.float32).astype(
        jnp.bfloat16
    )
    key_mask = jnp.broadcast_to(
        jnp.where(live_mask, 0.0, MASKED)[:, None], (token_count, TILE)
    ).astype(jnp.bfloat16)
    offsets = spread_table(table_low)
    attended, logs = attend(queries, keys_low, values_low, key_mask, offsets)
    middle = inputs + jnp.dot(attended, full_output, preferred_element_type=jnp.float32)
    second, second_inverse = rms_forward(middle, second_scale)
    second_low = second.astype(jnp.bfloat16)
    logits = jnp.dot(second_low, full_router, preferred_element_type=jnp.float32)
    router_probs = jax.nn.softmax(logits, axis=-1)
    choice_hot = expert_choice == jnp.arange(expert_count, dtype=jnp.int32)[None, :]
    gates = jnp.sum(jnp.where(choice_hot, router_probs, 0.0), axis=1)
    hot_live = (choice_hot & live_mask[:, None]).astype(jnp.int32)
    before = jnp.cumsum(hot_live, axis=0) - hot_live
    slot = jnp.sum(before * hot_live, axis=1)
    kept = live_mask & (slot < capacity)
    target = jnp.where(kept, expert_choice[:, 0] * capacity + slot, -1)
    dispatch = (
        target[None, :] == jnp.arange(expert_count * capacity, dtype=jnp.int32)[:, None]
    ).astype(jnp.bfloat16)

    def exchange(rows):
        return lax.all_to_all(
            rows.reshape(expert_count, capacity, model_width),
            "shard",
            split_axis=0,
            concat_axis=0,
            tiled=True,
        ).reshape(-1, model_width)

    send_rows = jnp.dot(dispatch, second_low, preferred_element_type=jnp.float32).astype(
        jnp.bfloat16
    )
    upstream = cotangent.astype(jnp.float32) * live_mask[:, None].astype(jnp.float32)
    result_grad = (gates[:, None] * upstream).astype(jnp.bfloat16)
    send_grad = jnp.dot(dispatch, result_grad, preferred_element_type=jnp.float32).astype(
        jnp.bfloat16
    )
    weight_in = expert_in[0]
    weight_out = expert_out[0]
    received = exchange(send_rows)
    arrived = exchange(send_grad)
    inner = jnp.dot(received, weight_in, preferred_element_type=jnp.float32)
    active_value, active_pull = jax.vjp(jax.nn.gelu, inner)
    active = active_value.astype(jnp.bfloat16)
    produced = jnp.dot(active, weight_out, preferred_element_type=jnp.float32).astype(jnp.bfloat16)
    returned = exchange(produced)
    out_weight_grad = contract(active, arrived, 0, 0).astype(jnp.bfloat16)
    out_total = replica_sum(out_weight_grad[None])
    active_grad = contract(arrived, weight_out, 1, 1)
    inner_grad = active_pull(active_grad)[0].astype(jnp.bfloat16)
    in_weight_grad = contract(received, inner_grad, 0, 0).astype(jnp.bfloat16)
    in_total = replica_sum(in_weight_grad[None])
    rows_grad = contract(inner_grad, weight_in, 1, 1).astype(jnp.bfloat16)
    rows_back = exchange(rows_grad)
    combined = contract(dispatch, returned, 0, 0)
    layer_out = (middle + gates[:, None] * combined).astype(jnp.bfloat16)
    gate_grad = jnp.sum(upstream * combined, axis=1)
    chosen_float = choice_hot.astype(jnp.float32)
    logit_grad = (
        router_probs * (chosen_float * gate_grad[:, None] - (gates * gate_grad)[:, None])
    ).astype(jnp.bfloat16)
    router_grad = contract(second_low, logit_grad, 0, 0)
    second_grad = contract(logit_grad, full_router, 1, 1) + contract(dispatch, rows_back, 0, 0)
    middle_part, second_gain_grad = rms_backward(middle, second_inverse, second_scale, second_grad)
    middle_grad = upstream + middle_part
    branch_grad = middle_grad.astype(jnp.bfloat16)
    output_grad = contract(attended, branch_grad, 0, 0)
    attended_grad = contract(branch_grad, full_output, 1, 1).astype(jnp.bfloat16)
    query_low, key_low, value_low, table_sums = attend_back(
        queries, keys_low, values_low, key_mask, offsets, logs, attended, attended_grad
    )
    table_grad = collect_table(table_sums, bucket_count)
    query_grad = contract(normed_low, query_low, 0, 0)
    key_grad = contract(normed_low, key_low, 0, 0)
    value_grad = contract(normed_low, value_low, 0, 0)
    normed_grad = (
        contract(query_low, full_query, 1, 1)
        + contract(key_low, full_key, 1, 1)
        + contract(value_low, full_value, 1, 1)
    )
    input_part, first_gain_grad = rms_backward(inputs, first_inverse, first_scale, normed_grad)
    token_grad = (middle_grad + input_part).astype(jnp.bfloat16)
    small_grads = (router_grad, first_gain_grad, second_gain_grad, table_grad)
    small_rows = jnp.concatenate(
        [grad.astype(jnp.bfloat16).reshape(group_size, -1) for grad in small_grads], axis=1
    )
    small_height = -(-small_rows.shape[1] // model_width)
    small_rows = jnp.pad(
        small_rows, ((0, 0), (0, small_height * model_width - small_rows.shape[1]))
    ).reshape(group_size, small_height, model_width)
    grads = jnp.concatenate(
        [
            grad.astype(jnp.bfloat16).reshape(group_size, shard_rows, model_width)
            for grad in (query_grad, key_grad, value_grad, output_grad)
        ]
        + [small_rows],
        axis=1,
    )
    group_sum = lax.psum_scatter(grads, "shard", scatter_dimension=0, tiled=True)
    group_sum, in_total, out_total = lax.optimization_barrier((group_sum, in_total, out_total))
    total = replica_sum(group_sum)[0].astype(jnp.float32)
    weight_totals = [
        total[index * shard_rows : (index + 1) * shard_rows] for index in range(4)
    ]
    flat = total[4 * shard_rows :].reshape(-1)
    small_totals = []
    position = 0
    for part in small_parts:
        small_totals.append(flat[position : position + part.size].reshape(part.shape))
        position += part.size
    router_total, first_total, second_total, table_total = small_totals
    return (
        layer_out,
        token_grad,
        *weight_totals,
        first_total,
        second_total,
        router_total,
        table_total,
        in_total.astype(jnp.float32),
        out_total.astype(jnp.float32),
    )


def solution(mesh):
    placed = (
        P(("shard", "rep"), None),
        P(("shard", "rep")),
        P(("shard", "rep"), None),
        P("shard", None),
        P("shard", None),
        P("shard", None),
        P("shard", None),
        P("shard"),
        P("shard"),
        P("shard", None),
        P("shard", None),
        P("shard", None, None),
        P("shard", None, None),
        P(("shard", "rep"), None),
    )
    return jax.shard_map(
        on_device,
        mesh=mesh,
        in_specs=placed,
        out_specs=(
            P(("shard", "rep"), None),
            P(("shard", "rep"), None),
            P("shard", None),
            P("shard", None),
            P("shard", None),
            P("shard", None),
            P("shard"),
            P("shard"),
            P("shard", None),
            P("shard", None),
            P("shard", None, None),
            P("shard", None, None),
        ),
        check_vma=False,
    )
```

```python
import jax
import jax.numpy as jnp
import numpy as np
from jax import lax
from jax.experimental import pallas as pl
from jax.experimental.pallas import tpu as pltpu
from jax.sharding import PartitionSpec as P

MAX_DISTANCE = 128
EPSILON = 1e-06
MASKED = -1000000000.0
TILE = 128
QUERY_BLOCK = 256


def contract(left_side, right_side, left_axis, right_axis):
    return lax.dot_general(
        left_side,
        right_side,
        (((left_axis,), (right_axis,)), ((), ())),
        preferred_element_type=jnp.float32,
    )


def offset_buckets(bucket_count, reach):
    half_count = bucket_count // 2
    exact_count = half_count // 2
    offset_list = -(np.arange(4 * TILE) - 2 * TILE)
    distance = np.abs(offset_list)
    spread_log = (
        np.log(np.maximum(distance, 1) / exact_count)
        / np.log(reach / exact_count)
        * (half_count - exact_count)
    )
    far_bucket = np.minimum(
        exact_count + np.maximum(spread_log, 0.0).astype(np.int64), half_count - 1
    )
    return (offset_list > 0) * half_count + np.where(
        distance < exact_count, distance, far_bucket
    )


def fill_strip(strip_ref, offsets, slot_count):
    base = slot_count - TILE
    wide = pltpu.roll(
        jnp.broadcast_to(offsets, (TILE, 4 * TILE)), 0, 1, stride=1, stride_axis=0
    )
    strip_ref[: base - TILE, :] = jnp.broadcast_to(
        offsets[:, 4 * TILE - 1 : 4 * TILE], (base - TILE, TILE)
    )
    for shift in (-1, 0, 1):
        first = (2 - shift) * TILE
        row = base + shift * TILE
        strip_ref[row : row + TILE, :] = wide[:, first : first + TILE]
    strip_ref[base + 2 * TILE :, :] = jnp.broadcast_to(
        offsets[:, 0:1], (slot_count - 2 * TILE, TILE)
    )


def biased(strip_ref, scores, first_row, slot_count):
    parts = []
    for part in range(QUERY_BLOCK // TILE):
        start = slot_count - TILE - first_row - part * TILE
        parts.append(
            scores[:, part * TILE : (part + 1) * TILE]
            + strip_ref[start : start + slot_count, :]
        )
    return jnp.concatenate(parts, axis=1)


def attend_kernel(q_ref, k_ref, v_ref, mask_ref, offset_ref, out_ref, log_ref, strip_ref):
    slot_count, width = q_ref.shape
    head_size = width // 2
    lane = lax.broadcasted_iota(jnp.int32, (QUERY_BLOCK, width), 1)
    one_lane = (lane == 0).astype(jnp.bfloat16)
    keys = jnp.concatenate([k_ref[...], mask_ref[...]], axis=1)
    values_turned = jnp.concatenate(
        [v_ref[...].T, jnp.ones((16, slot_count), jnp.bfloat16)], axis=0
    )
    for half in range(2):
        fill_strip(strip_ref.at[half], offset_ref[0, half : half + 1, :], slot_count)
    for first_row in range(0, slot_count, QUERY_BLOCK):
        rows = slice(first_row, first_row + QUERY_BLOCK)
        q_block = q_ref[rows, :] * jnp.bfloat16(0.125)
        pieces = []
        for half in range(2):
            mine = (lane // head_size) == half
            q_half = jnp.concatenate(
                [jnp.where(mine, q_block, jnp.bfloat16(0)), one_lane], axis=1
            )
            scores = biased(strip_ref.at[half], contract(keys, q_half, 1, 1), first_row, slot_count)
            peak = jnp.max(scores, axis=0, keepdims=True)
            weights = jnp.exp(scores - peak).astype(jnp.bfloat16)
            mixed = jnp.dot(values_turned, weights, preferred_element_type=jnp.float32)
            total = mixed[width : width + 1, :]
            pieces.append(mixed[half * head_size : (half + 1) * head_size, :] / total)
            log_ref[0, half : half + 1, rows] = peak + jnp.log(total)
        out_ref[rows, :] = jnp.concatenate(pieces, axis=0).T.astype(jnp.bfloat16)


def attend_back_kernel(
    q_ref, k_ref, v_ref, mask_ref, offset_ref, log_ref, out_ref, grad_ref,
    dq_ref, dk_ref, dv_ref, table_ref, strip_ref, sum_ref,
):
    slot_count, width = q_ref.shape
    head_size = width // 2
    lane = lax.broadcasted_iota(jnp.int32, (QUERY_BLOCK, width), 1)
    one_lane = (lane == 0).astype(jnp.bfloat16)
    keys = jnp.concatenate([k_ref[...], mask_ref[...]], axis=1)
    keys_turned = k_ref[...].T
    values = v_ref[...]
    for half in range(2):
        fill_strip(strip_ref.at[half], offset_ref[0, half : half + 1, :], slot_count)
    sum_ref[...] = jnp.zeros(sum_ref.shape, jnp.float32)
    key_total = jnp.zeros((slot_count, width), jnp.float32)
    value_total = jnp.zeros((slot_count, width), jnp.float32)
    for first_row in range(0, slot_count, QUERY_BLOCK):
        rows = slice(first_row, first_row + QUERY_BLOCK)
        q_block = q_ref[rows, :] * jnp.bfloat16(0.125)
        grad_block = grad_ref[rows, :]
        product = (
            grad_block.astype(jnp.float32) * out_ref[rows, :].astype(jnp.float32)
        ).T
        pieces = []
        weights_parts, score_parts, q_parts, grad_parts = [], [], [], []
        for half in range(2):
            mine = (lane // head_size) == half
            q_own = jnp.where(mine, q_block, jnp.bfloat16(0))
            grad_own = jnp.where(mine, grad_block, jnp.bfloat16(0))
            delta = jnp.sum(
                product[half * head_size : (half + 1) * head_size, :], axis=0, keepdims=True
            )
            q_half = jnp.concatenate([q_own, one_lane], axis=1)
            scores = biased(strip_ref.at[half], contract(keys, q_half, 1, 1), first_row, slot_count)
            weights = jnp.exp(scores - log_ref[0, half : half + 1, rows])
            prob_grad = contract(values, grad_own, 1, 1)
            score_grad = weights * (prob_grad - delta)
            for part in range(QUERY_BLOCK // TILE):
                start = slot_count - TILE - first_row - part * TILE
                sum_ref[half, start : start + slot_count, :] += score_grad[
                    :, part * TILE : (part + 1) * TILE
                ]
            score_low = score_grad.astype(jnp.bfloat16)
            turned = jnp.dot(keys_turned, score_low, preferred_element_type=jnp.float32)
            pieces.append(turned[half * head_size : (half + 1) * head_size, :] * 0.125)
            weights_parts.append(weights.astype(jnp.bfloat16))
            score_parts.append(score_low)
            q_parts.append(q_own)
            grad_parts.append(grad_own)
        dq_ref[rows, :] = jnp.concatenate(pieces, axis=0).T.astype(jnp.bfloat16)
        key_total = key_total + jnp.dot(
            jnp.concatenate(score_parts, axis=1),
            jnp.concatenate(q_parts, axis=0),
            preferred_element_type=jnp.float32,
        )
        value_total = value_total + jnp.dot(
            jnp.concatenate(weights_parts, axis=1),
            jnp.concatenate(grad_parts, axis=0),
            preferred_element_type=jnp.float32,
        )
    dk_ref[...] = key_total.astype(jnp.bfloat16)
    dv_ref[...] = value_total.astype(jnp.bfloat16)
    base = slot_count - TILE
    table_ref[...] = jnp.zeros(table_ref.shape, jnp.float32)
    for half in range(2):
        sums = sum_ref.at[half]
        wide = jnp.concatenate(
            [jnp.zeros((TILE, TILE), jnp.float32)]
            + [sums[base + shift * TILE : base + (shift + 1) * TILE, :] for shift in (1, 0, -1)],
            axis=1,
        )
        level = wide
        row = lax.broadcasted_iota(jnp.int32, wide.shape, 0)
        amount = 1
        while amount < TILE:
            level = jnp.where(
                (row // amount) % 2 == 1, pltpu.roll(level, 4 * TILE - amount, 1), level
            )
            amount *= 2
        table_ref[0, half : half + 1, :] = jnp.sum(level, axis=0, keepdims=True)
        far_left = jnp.sum(sums[: base - TILE, :], axis=0, keepdims=True)
        far_right = jnp.sum(sums[base + 2 * TILE :, :], axis=0, keepdims=True)
        table_ref[0, 2 + half : 3 + half, :] = jnp.concatenate(
            [far_left, far_right, jnp.zeros((1, 2 * TILE), jnp.float32)], axis=1
        )


def pair_specs(slot_count):
    column = pl.BlockSpec((slot_count, 2 * 64), lambda p: (0, p))
    mask = pl.BlockSpec((slot_count, TILE), lambda p: (0, 0))
    small = lambda rows, lanes: pl.BlockSpec((1, rows, lanes), lambda p: (p, 0, 0))
    return column, mask, small


def attend(queries, keys, values, mask, offsets):
    slot_count, model_width = queries.shape
    pairs = offsets.shape[0]
    column, mask_spec, small = pair_specs(slot_count)
    strip = pltpu.VMEM((2, 2 * slot_count - TILE, TILE), jnp.float32)
    return pl.pallas_call(
        attend_kernel,
        grid=(pairs,),
        in_specs=[column, column, column, mask_spec, small(2, 4 * TILE)],
        out_specs=[column, small(2, slot_count)],
        out_shape=[
            jax.ShapeDtypeStruct((slot_count, model_width), jnp.bfloat16),
            jax.ShapeDtypeStruct((pairs, 2, slot_count), jnp.float32),
        ],
        scratch_shapes=[strip],
        compiler_params=pltpu.CompilerParams(vmem_limit_bytes=50 * 2**20),
        cost_estimate=pl.CostEstimate(
            flops=2 * pairs * slot_count * slot_count * 800,
            bytes_accessed=8 * slot_count * model_width,
            transcendentals=2 * pairs * slot_count * slot_count,
        ),
        name="attend",
    )(queries, keys, values, mask, offsets)


def attend_back(queries, keys, values, mask, offsets, logs, attended, grad):
    slot_count, model_width = queries.shape
    pairs = offsets.shape[0]
    column, mask_spec, small = pair_specs(slot_count)
    strip = pltpu.VMEM((2, 2 * slot_count - TILE, TILE), jnp.float32)
    wide = jax.ShapeDtypeStruct((slot_count, model_width), jnp.bfloat16)
    return pl.pallas_call(
        attend_back_kernel,
        grid=(pairs,),
        in_specs=[
            column, column, column, mask_spec, small(2, 4 * TILE), small(2, slot_count),
            column, column,
        ],
        out_specs=[column, column, column, small(4, 4 * TILE)],
        out_shape=[
            wide, wide, wide, jax.ShapeDtypeStruct((pairs, 4, 4 * TILE), jnp.float32)
        ],
        scratch_shapes=[strip, strip],
        compiler_params=pltpu.CompilerParams(vmem_limit_bytes=56 * 2**20),
        cost_estimate=pl.CostEstimate(
            flops=2 * pairs * slot_count * slot_count * 1600,
            bytes_accessed=16 * slot_count * model_width,
            transcendentals=2 * pairs * slot_count * slot_count,
        ),
        name="attend_back",
    )(queries, keys, values, mask, offsets, logs, attended, grad)


def spread_table(table):
    bucket_count, head_count = table.shape
    hot = (
        offset_buckets(bucket_count, MAX_DISTANCE)[None, :] == np.arange(bucket_count)[:, None]
    )
    spread = contract(table, jnp.asarray(hot, jnp.bfloat16), 0, 0)
    return spread.reshape(head_count // 2, 2, 4 * TILE)


def collect_table(sums, bucket_count):
    pairs = sums.shape[0]
    buckets = offset_buckets(bucket_count, MAX_DISTANCE)
    near = sums[:, :2, :].reshape(2 * pairs, 4 * TILE)
    far = sums[:, 2:, : 2 * TILE].reshape(2 * pairs, 2 * TILE)
    hot = buckets[:, None] == np.arange(bucket_count)[None, :]
    far_buckets = np.where(np.arange(2 * TILE) < TILE, buckets[-1], buckets[0])
    far_hot = far_buckets[:, None] == np.arange(bucket_count)[None, :]
    both = jnp.concatenate([near, far], axis=1)
    both_hot = jnp.asarray(np.concatenate([hot, far_hot], axis=0), jnp.float32)
    return lax.dot_general(
        both_hot, both, (((0,), (1,)), ((), ())), precision=lax.Precision.HIGHEST,
        preferred_element_type=jnp.float32,
    )


def rms_forward(values, gain):
    inverse = lax.rsqrt(jnp.mean(values * values, axis=-1, keepdims=True) + EPSILON)
    return (values * inverse * gain, inverse)


def rms_backward(values, inverse, gain, upstream):
    scaled = upstream * gain
    gain_grad = jnp.sum(upstream * values * inverse, axis=0)
    inner_mean = jnp.mean(scaled * values, axis=-1, keepdims=True)
    return (inverse * scaled - values * inverse * inverse * inverse * inner_mean, gain_grad)


def pack_small(parts, width):
    flat = jnp.concatenate([part.reshape(-1) for part in parts])
    rows = -(-flat.shape[0] // width)
    return jnp.pad(flat, (0, rows * width - flat.shape[0])).reshape(rows, width)


def gather_packed(packed, group_size):
    replicas = lax.axis_size("rep")
    rows, width = packed.shape
    part = -(-rows // replicas)
    packed = jnp.pad(packed, ((0, part * replicas - rows), (0, 0)))
    own = lax.dynamic_slice_in_dim(packed, lax.axis_index("rep") * part, part, 0)
    whole = lax.all_gather(own, ("shard", "rep"), axis=0)
    return whole.reshape(group_size, part * replicas, width)[:, :rows]


def replica_sum(value):
    return lax.psum(value, "rep")


def on_device(
    tokens,
    lengths,
    expert_choice,
    query_weight,
    key_weight,
    value_weight,
    output_weight,
    first_gain,
    second_gain,
    router_weight,
    bias_table,
    expert_in,
    expert_out,
    cotangent,
):
    token_count, model_width = tokens.shape
    group_size = lax.axis_size("shard")
    expert_count = router_weight.shape[1]
    capacity = token_count // group_size
    bucket_count = bias_table.shape[0] * group_size
    shard_rows = query_weight.shape[0]
    live_mask = jnp.arange(token_count, dtype=jnp.int32) < lengths[0]
    small_parts = (router_weight, first_gain, second_gain, bias_table)
    packed = jnp.concatenate(
        [
            query_weight,
            key_weight,
            value_weight,
            pack_small(small_parts, model_width),
        ],
        axis=0,
    )
    whole = gather_packed(packed, group_size)
    whole, later_weight = lax.optimization_barrier((whole, output_weight))
    full_output = gather_packed(later_weight, group_size).reshape(-1, model_width)
    full_query, full_key, full_value = (
        whole[:, index * shard_rows : (index + 1) * shard_rows].reshape(-1, model_width)
        for index in range(3)
    )
    small = whole[:, 3 * shard_rows :].reshape(group_size, -1)
    unpacked = []
    position = 0
    for part in small_parts:
        unpacked.append(
            small[:, position : position + part.size].reshape((-1,) + part.shape[1:])
        )
        position += part.size
    full_router, first_low, second_low_gain, table_low = unpacked
    first_scale = first_low.astype(jnp.float32)
    second_scale = second_low_gain.astype(jnp.float32)
    inputs = tokens.astype(jnp.float32)
    normed, first_inverse = rms_forward(inputs, first_scale)
    normed_low = normed.astype(jnp.bfloat16)
    queries = jnp.dot(normed_low, full_query, preferred_element_type=jnp.float32).astype(
        jnp.bfloat16
    )
    keys_low = jnp.dot(normed_low, full_key, preferred_element_type=jnp.float32).astype(
        jnp.bfloat16
    )
    values_low = jnp.dot(normed_low, full_value, preferred_element_type=jnp.float32).astype(
        jnp.bfloat16
    )
    key_mask = jnp.broadcast_to(
        jnp.where(live_mask, 0.0, MASKED)[:, None], (token_count, TILE)
    ).astype(jnp.bfloat16)
    offsets = spread_table(table_low)
    attended, logs = attend(queries, keys_low, values_low, key_mask, offsets)
    middle = inputs + jnp.dot(attended, full_output, preferred_element_type=jnp.float32)
    second, second_inverse = rms_forward(middle, second_scale)
    second_low = second.astype(jnp.bfloat16)
    logits = jnp.dot(second_low, full_router, preferred_element_type=jnp.float32)
    router_probs = jax.nn.softmax(logits, axis=-1)
    choice_hot = expert_choice == jnp.arange(expert_count, dtype=jnp.int32)[None, :]
    gates = jnp.sum(jnp.where(choice_hot, router_probs, 0.0), axis=1)
    hot_live = (choice_hot & live_mask[:, None]).astype(jnp.int32)
    before = jnp.cumsum(hot_live, axis=0) - hot_live
    slot = jnp.sum(before * hot_live, axis=1)
    kept = live_mask & (slot < capacity)
    target = jnp.where(kept, expert_choice[:, 0] * capacity + slot, -1)
    dispatch = (
        target[None, :] == jnp.arange(expert_count * capacity, dtype=jnp.int32)[:, None]
    ).astype(jnp.bfloat16)

    def exchange(rows):
        return lax.all_to_all(
            rows.reshape(expert_count, capacity, model_width),
            "shard",
            split_axis=0,
            concat_axis=0,
            tiled=True,
        ).reshape(-1, model_width)

    send_rows = jnp.dot(dispatch, second_low, preferred_element_type=jnp.float32).astype(
        jnp.bfloat16
    )
    upstream = cotangent.astype(jnp.float32) * live_mask[:, None].astype(jnp.float32)
    result_grad = (gates[:, None] * upstream).astype(jnp.bfloat16)
    send_grad = jnp.dot(dispatch, result_grad, preferred_element_type=jnp.float32).astype(
        jnp.bfloat16
    )
    weight_in = expert_in[0]
    weight_out = expert_out[0]
    received = exchange(send_rows)
    arrived = exchange(send_grad)
    inner = jnp.dot(received, weight_in, preferred_element_type=jnp.float32)
    active_value, active_pull = jax.vjp(jax.nn.gelu, inner)
    active = active_value.astype(jnp.bfloat16)
    produced = jnp.dot(active, weight_out, preferred_element_type=jnp.float32).astype(jnp.bfloat16)
    returned = exchange(produced)
    out_weight_grad = contract(active, arrived, 0, 0).astype(jnp.bfloat16)
    out_total = replica_sum(out_weight_grad[None])
    active_grad = contract(arrived, weight_out, 1, 1)
    inner_grad = active_pull(active_grad)[0].astype(jnp.bfloat16)
    in_weight_grad = contract(received, inner_grad, 0, 0).astype(jnp.bfloat16)
    in_part = lax.psum_scatter(in_weight_grad[None], "rep", scatter_dimension=1, tiled=True)
    in_total = lax.all_gather(in_part, "rep", axis=1, tiled=True)
    rows_grad = contract(inner_grad, weight_in, 1, 1).astype(jnp.bfloat16)
    rows_back = exchange(rows_grad)
    combined = contract(dispatch, returned, 0, 0)
    layer_out = (middle + gates[:, None] * combined).astype(jnp.bfloat16)
    gate_grad = jnp.sum(upstream * combined, axis=1)
    chosen_float = choice_hot.astype(jnp.float32)
    logit_grad = (
        router_probs * (chosen_float * gate_grad[:, None] - (gates * gate_grad)[:, None])
    ).astype(jnp.bfloat16)
    router_grad = contract(second_low, logit_grad, 0, 0)
    second_grad = contract(logit_grad, full_router, 1, 1) + contract(dispatch, rows_back, 0, 0)
    middle_part, second_gain_grad = rms_backward(middle, second_inverse, second_scale, second_grad)
    middle_grad = upstream + middle_part
    branch_grad = middle_grad.astype(jnp.bfloat16)
    output_grad = contract(attended, branch_grad, 0, 0)
    attended_grad = contract(branch_grad, full_output, 1, 1).astype(jnp.bfloat16)
    query_low, key_low, value_low, table_sums = attend_back(
        queries, keys_low, values_low, key_mask, offsets, logs, attended, attended_grad
    )
    table_grad = collect_table(table_sums, bucket_count)
    query_grad = contract(normed_low, query_low, 0, 0)
    key_grad = contract(normed_low, key_low, 0, 0)
    value_grad = contract(normed_low, value_low, 0, 0)
    normed_grad = (
        contract(query_low, full_query, 1, 1)
        + contract(key_low, full_key, 1, 1)
        + contract(value_low, full_value, 1, 1)
    )
    input_part, first_gain_grad = rms_backward(inputs, first_inverse, first_scale, normed_grad)
    token_grad = (middle_grad + input_part).astype(jnp.bfloat16)
    small_grads = (router_grad, first_gain_grad, second_gain_grad, table_grad)
    small_rows = jnp.concatenate(
        [grad.astype(jnp.bfloat16).reshape(group_size, -1) for grad in small_grads], axis=1
    )
    small_height = -(-small_rows.shape[1] // model_width)
    small_rows = jnp.pad(
        small_rows, ((0, 0), (0, small_height * model_width - small_rows.shape[1]))
    ).reshape(group_size, small_height, model_width)
    grads = jnp.concatenate(
        [
            grad.astype(jnp.bfloat16).reshape(group_size, shard_rows, model_width)
            for grad in (query_grad, key_grad, value_grad, output_grad)
        ]
        + [small_rows],
        axis=1,
    )
    group_sum = lax.psum_scatter(grads, "shard", scatter_dimension=0, tiled=True)
    group_sum, in_total, out_total = lax.optimization_barrier((group_sum, in_total, out_total))
    total = replica_sum(group_sum)[0].astype(jnp.float32)
    weight_totals = [
        total[index * shard_rows : (index + 1) * shard_rows] for index in range(4)
    ]
    flat = total[4 * shard_rows :].reshape(-1)
    small_totals = []
    position = 0
    for part in small_parts:
        small_totals.append(flat[position : position + part.size].reshape(part.shape))
        position += part.size
    router_total, first_total, second_total, table_total = small_totals
    return (
        layer_out,
        token_grad,
        *weight_totals,
        first_total,
        second_total,
        router_total,
        table_total,
        in_total.astype(jnp.float32),
        out_total.astype(jnp.float32),
    )


def solution(mesh):
    placed = (
        P(("shard", "rep"), None),
        P(("shard", "rep")),
        P(("shard", "rep"), None),
        P("shard", None),
        P("shard", None),
        P("shard", None),
        P("shard", None),
        P("shard"),
        P("shard"),
        P("shard", None),
        P("shard", None),
        P("shard", None, None),
        P("shard", None, None),
        P(("shard", "rep"), None),
    )
    return jax.shard_map(
        on_device,
        mesh=mesh,
        in_specs=placed,
        out_specs=(
            P(("shard", "rep"), None),
            P(("shard", "rep"), None),
            P("shard", None),
            P("shard", None),
            P("shard", None),
            P("shard", None),
            P("shard"),
            P("shard"),
            P("shard", None),
            P("shard", None),
            P("shard", None, None),
            P("shard", None, None),
        ),
        check_vma=False,
    )
```
